32 devices in a mesh: groups: 2 (over x), region: 16 (over z, y, core).
Axes of the slice: x: 2, y: 2, z: 4, core: 2. Of those that a mesh axis runs over, the one named last changes fastest.
Arguments:
- successor: int32 [4, 262144], P(None, ('groups', 'region')), parts along dimension 1, may hold values from 0 to 12287, as said below
- send_rows: int32 [32, 16, 256], P(('groups', 'region')), parts along dimension 0, may hold values from 0 to 8191, as said below
- rewards: float32 [4, 262144], P(None, ('groups', 'region')), parts along dimension 1, may hold values from -3 to -0.2
- value_init: float32 [16, 262144], P(None, ('groups', 'region')), parts along dimension 1, may hold values from -6 to 6
- start_mass: float32 [16, 262144], P(None, ('groups', 'region')), parts along dimension 1, may hold values from 0 to 1
- dest: int32 [32], P('groups'), parts along dimension 0, may hold values from 0 to 131071
Outputs:
- values: float32 [16, 262144], P(None, ('groups', 'region')), parts along dimension 1
- edge_visits: float32 [4, 262144], P(None, ('groups', 'region')), parts along dimension 1
- arrival: float32 [16, 262144], P(None, ('groups', 'region')), parts along dimension 1
- log_partition: float32 [32], P('groups'), parts along dimension 0
The draws below stay inside these ranges and needn't reach their ends.
There are 2 independent parts, one for each index of `groups`. The reference program is written for one: setup_inputs(seed, part) draws one part's arguments, and reference() takes and returns one part's arrays. A program takes and returns all parts, laid end to end along the dimension named above; each array names one. Nothing has to cross between parts.
Inputs may be any that keep to these rules, and one draw needn't show every extreme that they name: `successor`: every index below 8192 names an own segment; a boundary slot 8192 + i * 256 + b is named only where b is below the live count of peer i, which is at least 1. `send_rows`: local segment rows; slots past the live count are padding and not read by any edge.
All inputs are finite; a program needn't handle non-finite values.
Results may differ from the reference program's by a relative error of at most 0.00002.
Values sent between devices are 32-bit elements; how exact they have to be, the bound alone decides.
A program may use at most 128 MiB of HBM per device.

```python
import jax
import jax.numpy as jnp

K = 16
DEG = 4
S_DEV = 8192
B = 256
S = 131072
N_REGION = 16


def live_counts(key):
    key = jax.random.fold_in(key, 11)
    first, second = jax.random.split(key)
    counts = jax.random.randint(first, (N_REGION, N_REGION), 1, B + 1)
    full_peer = jax.random.randint(second, (N_REGION,), 0, N_REGION)
    peers = jnp.arange(N_REGION, dtype=jnp.int32)[None, :]
    return jnp.where(peers == full_peer[:, None], B, counts).astype(jnp.int32)


def draw_successor(key, part):
    counts = live_counts(key)
    key = jax.random.fold_in(key, 5)
    keys = jax.random.split(key, 4)
    local = jax.random.randint(keys[0], (DEG, S), 0, S_DEV)
    remote_flag = jax.random.randint(keys[1], (DEG, S), 0, 4) == 0
    source = jax.random.randint(keys[2], (DEG, S), 0, N_REGION)
    owner = jnp.broadcast_to((jnp.arange(S, dtype=jnp.int32) // S_DEV)[None, :], (DEG, S))
    live = counts[source, owner]
    slot = jax.random.randint(keys[3], (DEG, S), 0, 1048576) % live
    ghost = S_DEV + source * B + slot
    return jnp.where(remote_flag, ghost, local).astype(jnp.int32)


def draw_send_rows(key, part):
    key = jax.random.fold_in(key, 7)
    return jax.random.randint(key, (N_REGION, N_REGION, B), 0, S_DEV).astype(jnp.int32)


def with_ends(drawn, rng, low, largest):
    longest = drawn.shape.index(max(drawn.shape))
    spots = []
    for shift in (0, 1):
        where = [jax.random.randint(jax.random.fold_in(rng, axis), (), 0, length) for axis, length in enumerate(drawn.shape)]
        where[longest] = (where[longest] + shift) % drawn.shape[longest]
        spots.append(tuple(where))
    return drawn.at[spots[0]].set(low).at[spots[1]].set(largest)


def steps_of(stream_key, shape, shards, smallest, largest):
    def one(axis_at, parts):
        draws = jax.random.uniform(jax.random.fold_in(jax.random.fold_in(stream_key, 6), axis_at), (parts,), jnp.float32, smallest / len(shards), largest / len(shards))
        return jnp.repeat(jnp.exp(draws), shape[axis_at] // parts).reshape((-1,) + (1,) * (len(shape) - axis_at - 1))

    gain = one(*shards[0])
    for cut in shards[1:]:
        gain = gain * one(*cut)
    return gain


def gaussian(rng, shape, spread, most, cuts=(), held_as=jnp.bfloat16):
    entries = spread * jax.random.normal(rng, shape, jnp.float32)
    if cuts:
        entries = entries * steps_of(rng, shape, cuts, -0.22, 0.18)
    return jnp.clip(entries, -most, most).astype(held_as)


def setup_inputs(seed: int = 0, part: int = 0) -> dict:
    key_list = jax.random.split(jax.random.key(seed), 7)
    own_keys = jax.random.split(jax.random.fold_in(key_list[6], part), 7)
    successor = draw_successor(jax.random.fold_in(jax.random.fold_in(key_list[6], part), 71), part)
    send_rows = draw_send_rows(jax.random.fold_in(jax.random.fold_in(key_list[6], part), 71), part)
    rewards = jnp.clip(-3.0 + 2.8 * jax.random.uniform(own_keys[2], (DEG, S), jnp.float32) ** steps_of(own_keys[2], (DEG, S), ((1, 16),), -0.2, 0.2), -3.0, -0.2)
    value_init = gaussian(own_keys[3], (K, S), 1.0, 6.0, ((1, 16),), jnp.float32)
    start_mass = jnp.clip(1.0 * jax.random.uniform(own_keys[4], (K, S), jnp.float32) ** steps_of(own_keys[4], (K, S), ((1, 16),), -0.2, 0.2), 0.0, 1.0)
    dest = with_ends(jax.random.randint(own_keys[5], (K,), 0, S), jax.random.fold_in(own_keys[5], 1), 0, S - 1).astype(jnp.int32)
    return dict(successor=successor, send_rows=send_rows, rewards=rewards, value_init=value_init, start_mass=start_mass, dest=dest)


def global_successor(successor, send_rows):
    peers = jnp.arange(N_REGION, dtype=jnp.int32)
    ghost_map = jnp.transpose(send_rows, (1, 0, 2)) + (peers * S_DEV)[None, :, None]
    ghost_map = ghost_map.reshape(N_REGION, N_REGION * B)
    owner = (jnp.arange(S, dtype=jnp.int32) // S_DEV)[None, :]
    owner = jnp.broadcast_to(owner, successor.shape)
    slot = jnp.clip(successor - S_DEV, 0, N_REGION * B - 1)
    remote = ghost_map[owner, slot]
    return jnp.where(successor < S_DEV, owner * S_DEV + successor, remote).astype(jnp.int32)


def reference(successor, send_rows, rewards, value_init, start_mass, dest):
    target = global_successor(successor, send_rows)
    is_dest = jnp.arange(S, dtype=jnp.int32)[None, :] == dest[:, None]

    def backup(value):
        q_value = rewards[None] + value[:, target]
        new_value = jnp.log(jnp.sum(jnp.exp(q_value), axis=1))
        return jnp.where(is_dest, jnp.float32(0.0), new_value), q_value

    first, _ = backup(value_init)
    values, q_value = backup(first)
    policy = jnp.exp(q_value - values[:, None])
    policy = jnp.where(is_dest[:, None], jnp.float32(0.0), policy)

    def push(mass):
        flow = mass[:, None] * policy
        return jnp.zeros((K, S), jnp.float32).at[:, target].add(flow)

    mass_one = push(start_mass)
    arrival = push(mass_one)
    edge_visits = jnp.sum((start_mass + mass_one)[:, None] * policy, axis=0)
    log_partition = jnp.sum(start_mass * values, axis=1)
    return values, edge_visits, arrival, log_partition
```

```python
import functools

import jax
import jax.numpy as jnp
from jax import lax
from jax.experimental import pallas as pl
from jax.experimental.pallas import tpu as pltpu
from jax.sharding import PartitionSpec as P

LANES = 128
VMEM = pl.BlockSpec(memory_space=pltpu.VMEM)
SMEM = pl.BlockSpec(memory_space=pltpu.SMEM)
TABLES = 2


def group_of(rows, dests):
    return lax.broadcasted_iota(jnp.int32, (rows, LANES), 1) // dests


def fold(x, dests):
    shift = dests
    while shift < LANES:
        x = x + pltpu.roll(x, shift, axis=1)
        shift *= 2
    return x


def rows_of(block):
    return jnp.concatenate([block] * (LANES // block.shape[0]), axis=0).T


def ds(start, size):
    return pl.ds(pl.multiple_of(start, size), size)


def pack_send(table, send_rows, out, dests):
    _, peers, slots = send_rows.shape
    groups = LANES // dests
    per = slots // groups
    where = group_of(1, dests)

    @pl.loop(0, peers)
    def _(i):
        @pl.loop(0, per, unroll=4)
        def _(r):
            row = table[pl.ds(send_rows[0, i, r], 1), :]
            for c in range(1, groups):
                other = table[pl.ds(send_rows[0, i, c * per + r], 1), :]
                row = jnp.where(where == c, other, row)
            out[pl.ds(i * per + r, 1), :] = row


def fill(table, own, received, peers, slots, dests):
    seg = own.shape[0]
    groups = LANES // dests
    per = slots // groups
    where = group_of(per, dests)

    @pl.loop(0, seg // 64, unroll=2)
    def _(b):
        table[ds(b * 64, 64), :] = own[ds(b * 64, 64), :]

    @pl.loop(0, peers)
    def _(i):
        block = received[ds(i * per, per), :]
        for c in range(groups):
            one = fold(jnp.where(where == c, block, 0.0), dests)
            table[ds(seg + i * slots + c * per, per), :] = one


def gather(table, successor, out, dests):
    edges, seg = successor.shape
    half = seg // 2
    where = group_of(1, dests)

    @pl.loop(0, half, unroll=4)
    def _(r):
        row = None
        for c in range(2 * edges):
            other = table[pl.ds(successor[c % edges, r + (c // edges) * half], 1), :]
            row = other if row is None else jnp.where(where == c, other, row)
        out[pl.ds(r, 1), :] = row


def scatter(tables, flow, successor, dests):
    edges, seg = successor.shape
    half = seg // 2
    step = half // len(tables)
    where = group_of(1, dests)

    for table in tables:
        @pl.loop(0, table.shape[0] // 64)
        def _(b):
            table[ds(b * 64, 64), :] = jnp.zeros((64, LANES), jnp.float32)

    @pl.loop(0, step, unroll=2)
    def _(r0):
        work = []
        for n, table in enumerate(tables):
            r = r0 + n * step
            row = flow[pl.ds(r, 1), :]
            for c in range(2 * edges):
                at = table.at[pl.ds(successor[c % edges, r + (c // edges) * half], 1), :]
                work.append((at, at[...] + row, where == c))
        for at, value, mask in work:
            pltpu.store(at, value, mask=mask)


def settle(table, received, send_rows, dests):
    _, peers, slots = send_rows.shape
    groups = LANES // dests
    per = slots // groups
    where = group_of(1, dests)

    @pl.loop(0, peers)
    def _(i):
        @pl.loop(0, per, unroll=2)
        def _(r):
            row = received[pl.ds(i * per + r, 1), :]
            work = []
            for c in range(groups):
                at = table.at[pl.ds(send_rows[0, i, c * per + r], 1), :]
                work.append((at, at[...] + row, where == c))
            for at, value, mask in work:
                pltpu.store(at, value, mask=mask)


def total(tables, rows):
    x = tables[0][rows, :]
    for table in tables[1:]:
        x = x + table[rows, :]
    return x


def finish_spread(tables, seg, peers, slots, own_out, send_out, dests):
    groups = LANES // dests
    per = slots // groups
    where = group_of(per, dests)

    @pl.loop(0, seg // 64)
    def _(b):
        own_out[ds(b * 64, 64), :] = total(tables, ds(b * 64, 64))

    @pl.loop(0, peers)
    def _(i):
        block = None
        for c in range(groups):
            one = fold(total(tables, ds(seg + i * slots + c * per, per)), dests)
            block = one if block is None else jnp.where(where == c, one, block)
        send_out[i, pl.ds(0, per), :] = block


def start_kernel(value, send_rows, table, send):
    dests, seg = value.shape

    @pl.loop(0, seg // LANES, unroll=2)
    def _(b):
        table[ds(b * LANES, LANES), :] = rows_of(jnp.exp(value[:, ds(b * LANES, LANES)]))

    pack_send(table, send_rows, send, dests)


def first_kernel(own, received, successor, rewards, dest_at, send_rows, new, weight, send, table, got):
    edges, seg = successor.shape
    _, peers, slots = send_rows.shape
    half = seg // 2
    dests = LANES // (2 * edges)
    fill(table, own, received, peers, slots, dests)
    gather(table, successor, got, dests)
    lane = lax.broadcasted_iota(jnp.int32, (LANES, LANES), 1)
    line = lax.broadcasted_iota(jnp.int32, (LANES, LANES), 0)

    @pl.loop(0, half // LANES)
    def _(b):
        at = ds(b * LANES, LANES)
        both = [jnp.exp(rewards[:, ds(h * half + b * LANES, LANES)]) for h in range(2)]
        lines = [jnp.broadcast_to(x[e : e + 1, :], (dests, LANES)) for x in both for e in range(edges)]
        w = jnp.concatenate(lines, axis=0).T
        weight[at, :] = w
        p = got[at, :] * w
        for h in range(2):
            mine = (lane >= LANES // 2) == (h == 1)
            x = fold(jnp.where(mine, p, 0.0), dests)
            is_dest = line + (h * half + b * LANES) == dest_at[...]
            new[ds(h * half + b * LANES, LANES), :] = jnp.where(is_dest, 1.0, x)

    pack_send(new, send_rows, send, dests)


def second_kernel(own, received, successor, weight, dest_at, start_mass, peers, slots,
                  values, p_out, inverse, landed, send, table, flow, *more):
    edges, seg = successor.shape
    half = seg // 2
    dests = LANES // (2 * edges)
    fill(table, own, received, peers, slots, dests)
    gather(table, successor, p_out, dests)
    lane = lax.broadcasted_iota(jnp.int32, (LANES, LANES), 1)
    line = lax.broadcasted_iota(jnp.int32, (LANES, LANES), 0)

    def body(b, weighted):
        at = ds(b * LANES, LANES)
        w = weight[at, :]
        p = p_out[at, :] * w
        p_out[at, :] = p
        parts = []
        for h in range(2):
            here = ds(h * half + b * LANES, LANES)
            mine = (lane >= LANES // 2) == (h == 1)
            x = fold(jnp.where(mine, p, 0.0), dests)
            is_dest = line + (h * half + b * LANES) == dest_at[...]
            v = jnp.where(is_dest, 0.0, jnp.log(x)).T[:dests, :]
            values[:, here] = v
            mass = start_mass[:, here]
            weighted = weighted + mass * v
            inv = jnp.where(is_dest, 0.0, 1.0 / x)
            inverse[here, :] = inv
            parts.append(rows_of(mass) * inv)
        flow[at, :] = jnp.where(lane >= LANES // 2, parts[1], parts[0]) * w
        return weighted

    weighted = lax.fori_loop(0, half // LANES, body, jnp.zeros((dests, LANES), jnp.float32))
    tables = (table,) + more
    scatter(tables, flow, successor, dests)
    finish_spread(tables, seg, peers, slots, landed, send, dests)
    per = slots * dests // LANES

    @pl.loop(0, peers)
    def _(i):
        send[i, pl.ds(per, dests), :] = weighted


def third_kernel(own, received, successor, weight, start_mass, p_in, inverse, landed_in, send_rows,
                 edge_visits, landed, send, total_out, table, flow, inward, *more):
    edges, seg = successor.shape
    _, peers, slots = send_rows.shape
    half = seg // 2
    dests = LANES // (2 * edges)
    per = slots * dests // LANES
    lane = lax.broadcasted_iota(jnp.int32, (LANES, LANES), 1)

    weighted = jnp.zeros((dests, LANES), jnp.float32)
    for i in range(peers):
        inward[pl.ds(i * per, per), :] = received[i, :per, :]
        weighted = weighted + received[i, per:, :]
    total_out[...] = jnp.broadcast_to(jnp.sum(weighted, axis=1, keepdims=True), (dests, LANES))

    @pl.loop(0, seg // 64)
    def _(b):
        table[ds(b * 64, 64), :] = landed_in[ds(b * 64, 64), :]

    settle(table, inward, send_rows, dests)

    @pl.loop(0, half // LANES)
    def _(b):
        at = ds(b * LANES, LANES)
        visits, parts = [], []
        for h in range(2):
            here = ds(h * half + b * LANES, LANES)
            mass = own[here, :] * fold(table[here, :], dests)
            inv = inverse[here, :]
            parts.append(mass * inv)
            visits.append((rows_of(start_mass[:, here]) + mass) * inv)
        flow[at, :] = jnp.where(lane >= LANES // 2, parts[1], parts[0]) * weight[at, :]
        seen = jnp.where(lane >= LANES // 2, visits[1], visits[0]) * p_in[at, :]
        seen = seen.T
        lines = [jnp.sum(seen[c * dests : (c + 1) * dests, :], axis=0, keepdims=True) for c in range(2 * edges)]
        for h in range(2):
            edge_visits[:, ds(h * half + b * LANES, LANES)] = jnp.concatenate(
                lines[h * edges : (h + 1) * edges], axis=0
            )

    tables = (table,) + more
    scatter(tables, flow, successor, dests)
    finish_spread(tables, seg, peers, slots, landed, send, dests)


def last_kernel(own, received, landed_in, send_rows, arrival, table):
    dests, seg = arrival.shape

    @pl.loop(0, seg // 64)
    def _(b):
        table[ds(b * 64, 64), :] = landed_in[ds(b * 64, 64), :]

    settle(table, received, send_rows, dests)

    @pl.loop(0, seg // LANES)
    def _(b):
        at = ds(b * LANES, LANES)
        arrival[:, at] = (own[at, :] * fold(table[at, :], dests)).T[:dests, :]


def call(kernel, specs, shapes, scratch, name):
    return pl.pallas_call(
        kernel,
        in_specs=specs,
        out_specs=[VMEM] * len(shapes),
        out_shape=[jax.ShapeDtypeStruct(s, jnp.float32) for s in shapes],
        scratch_shapes=[pltpu.VMEM(s, jnp.float32) for s in scratch],
        compiler_params=pltpu.CompilerParams(vmem_limit_bytes=56 * 1024 * 1024),
        name=name,
    )


def local(successor, send_rows, rewards, value_init, start_mass, dest):
    edges, seg = successor.shape
    _, peers, slots = send_rows.shape
    dests = value_init.shape[0]
    half = seg // 2
    groups = LANES // dests
    per = slots // groups
    all_rows = seg + peers * slots
    dest_at = jnp.tile(dest - lax.axis_index("region") * seg, groups)[None]
    rows, packed, sent = (seg, LANES), (half, LANES), (peers * per, LANES)
    big = (all_rows, LANES)
    more = [big] * (TABLES - 1)

    def exchange(x):
        y = lax.all_to_all(
            x.reshape(peers, -1, LANES), "region", split_axis=0, concat_axis=0, tiled=True
        )
        return y.reshape(x.shape)

    zero, send = call(start_kernel, [VMEM, SMEM], [rows, sent], [], "start")(value_init, send_rows)
    one, weight, send = call(
        first_kernel, [VMEM, VMEM, SMEM, VMEM, VMEM, SMEM], [rows, packed, sent], [big, packed], "first"
    )(zero, exchange(send), successor, rewards, dest_at, send_rows)

    def second(own, received, succ, w, d, mass, *rest):
        second_kernel(own, received, succ, w, d, mass, peers, slots, *rest)

    values, p, inverse, landed, send = call(
        second, [VMEM, VMEM, SMEM, VMEM, VMEM, VMEM],
        [(dests, seg), packed, rows, rows, (peers, per + dests, LANES)], [big, packed] + more, "second",
    )(one, exchange(send), successor, weight, dest_at, start_mass)
    edge_visits, landed, send, totals = call(
        third_kernel, [VMEM, VMEM, SMEM, VMEM, VMEM, VMEM, VMEM, VMEM, SMEM],
        [(edges, seg), rows, (peers, per, LANES), (dests, LANES)], [big, packed, sent] + more, "third",
    )(one, exchange(send), successor, weight, start_mass, p, inverse, landed, send_rows)
    (arrival,) = call(last_kernel, [VMEM, VMEM, VMEM, SMEM], [(dests, seg)], [rows], "last")(
        one, exchange(send).reshape(sent), landed, send_rows
    )
    return values, edge_visits, arrival, totals[:, 0]


def solution(mesh):
    placed = (
        P(None, ("groups", "region")),
        P(("groups", "region"), None, None),
        P(None, ("groups", "region")),
        P(None, ("groups", "region")),
        P(None, ("groups", "region")),
        P("groups"),
    )
    return jax.shard_map(
        local,
        mesh=mesh,
        in_specs=placed,
        out_specs=(
            P(None, ("groups", "region")),
            P(None, ("groups", "region")),
            P(None, ("groups", "region")),
            P("groups"),
        ),
        check_vma=False,
    )
```

```python
import functools

import jax
import jax.numpy as jnp
from jax import lax
from jax.experimental import pallas as pl
from jax.experimental.pallas import tpu as pltpu
from jax.sharding import PartitionSpec as P

LANES = 128
VMEM = pl.BlockSpec(memory_space=pltpu.VMEM)
SMEM = pl.BlockSpec(memory_space=pltpu.SMEM)
TABLES = 2


def group_of(rows, dests):
    return lax.broadcasted_iota(jnp.int32, (rows, LANES), 1) // dests


def fold(x, dests):
    shift = dests
    while shift < LANES:
        x = x + pltpu.roll(x, shift, axis=1)
        shift *= 2
    return x


def rows_of(block):
    return jnp.concatenate([block] * (LANES // block.shape[0]), axis=0).T


def ds(start, size):
    return pl.ds(pl.multiple_of(start, size), size)


def pack_send(table, send_rows, out, dests, peers):
    slots = send_rows.shape[0] // peers
    groups = LANES // dests
    per = slots // groups
    where = group_of(1, dests)

    @pl.loop(0, peers)
    def _(i):
        @pl.loop(0, per, unroll=8)
        def _(r):
            row = table[pl.ds(send_rows[i * slots + r], 1), :]
            for c in range(1, groups):
                other = table[pl.ds(send_rows[i * slots + c * per + r], 1), :]
                row = jnp.where(where == c, other, row)
            out[pl.ds(i * per + r, 1), :] = row


def fill(table, own, received, peers, slots, dests):
    seg = own.shape[0]
    groups = LANES // dests
    per = slots // groups
    where = group_of(per, dests)

    @pl.loop(0, seg // 64, unroll=2)
    def _(b):
        table[ds(b * 64, 64), :] = own[ds(b * 64, 64), :]

    @pl.loop(0, peers)
    def _(i):
        block = received[ds(i * per, per), :]
        for c in range(groups):
            one = fold(jnp.where(where == c, block, 0.0), dests)
            table[ds(seg + i * slots + c * per, per), :] = one


def gather(table, successor, out, dests):
    half = out.shape[0]
    edges = LANES // (2 * dests)
    where = group_of(1, dests)

    @pl.loop(0, half, unroll=8)
    def _(r):
        row = None
        for c in range(2 * edges):
            other = table[pl.ds(successor[(c % edges * 2 + c // edges) * half + r], 1), :]
            row = other if row is None else jnp.where(where == c, other, row)
        out[pl.ds(r, 1), :] = row


def scatter(tables, flow, successor, dests):
    half = flow.shape[0]
    edges = LANES // (2 * dests)
    step = half // len(tables)
    where = group_of(1, dests)

    for table in tables:
        @pl.loop(0, table.shape[0] // 64)
        def _(b):
            table[ds(b * 64, 64), :] = jnp.zeros((64, LANES), jnp.float32)

    @pl.loop(0, step, unroll=2)
    def _(r0):
        work = []
        for n, table in enumerate(tables):
            r = r0 + n * step
            row = flow[pl.ds(r, 1), :]
            for c in range(2 * edges):
                at = table.at[pl.ds(successor[(c % edges * 2 + c // edges) * half + r], 1), :]
                work.append((at, at[...] + row, where == c))
        for at, value, mask in work:
            pltpu.store(at, value, mask=mask)


def settle(table, received, send_rows, dests, peers):
    slots = send_rows.shape[0] // peers
    groups = LANES // dests
    per = slots // groups
    where = group_of(1, dests)

    @pl.loop(0, peers)
    def _(i):
        @pl.loop(0, per, unroll=4)
        def _(r):
            row = received[pl.ds(i * per + r, 1), :]
            work = []
            for c in range(groups):
                at = table.at[pl.ds(send_rows[i * slots + c * per + r], 1), :]
                work.append((at, at[...] + row, where == c))
            for at, value, mask in work:
                pltpu.store(at, value, mask=mask)


def total(tables, rows):
    x = tables[0][rows, :]
    for table in tables[1:]:
        x = x + table[rows, :]
    return x


def finish_spread(tables, seg, peers, slots, own_out, send_out, dests):
    groups = LANES // dests
    per = slots // groups
    where = group_of(per, dests)

    @pl.loop(0, seg // 64)
    def _(b):
        own_out[ds(b * 64, 64), :] = total(tables, ds(b * 64, 64))

    @pl.loop(0, peers)
    def _(i):
        block = None
        for c in range(groups):
            one = fold(total(tables, ds(seg + i * slots + c * per, per)), dests)
            block = one if block is None else jnp.where(where == c, one, block)
        send_out[i, pl.ds(0, per), :] = block


def start_kernel(peers, value, send_rows, table, send):
    dests, seg = value.shape

    @pl.loop(0, seg // LANES, unroll=2)
    def _(b):
        table[ds(b * LANES, LANES), :] = rows_of(jnp.exp(value[:, ds(b * LANES, LANES)]))

    pack_send(table, send_rows, send, dests, peers)


def first_kernel(peers, own, received, successor, rewards, dest_at, send_rows, new, weight, send, table, got):
    edges, seg = rewards.shape
    slots = send_rows.shape[0] // peers
    half = seg // 2
    dests = LANES // (2 * edges)
    fill(table, own, received, peers, slots, dests)
    gather(table, successor, got, dests)
    lane = lax.broadcasted_iota(jnp.int32, (LANES, LANES), 1)
    line = lax.broadcasted_iota(jnp.int32, (LANES, LANES), 0)

    @pl.loop(0, half // LANES)
    def _(b):
        at = ds(b * LANES, LANES)
        both = [jnp.exp(rewards[:, ds(h * half + b * LANES, LANES)]) for h in range(2)]
        lines = [jnp.broadcast_to(x[e : e + 1, :], (dests, LANES)) for x in both for e in range(edges)]
        w = jnp.concatenate(lines, axis=0).T
        weight[at, :] = w
        p = got[at, :] * w
        for h in range(2):
            mine = (lane >= LANES // 2) == (h == 1)
            x = fold(jnp.where(mine, p, 0.0), dests)
            is_dest = line + (h * half + b * LANES) == dest_at[...]
            new[ds(h * half + b * LANES, LANES), :] = jnp.where(is_dest, 1.0, x)

    pack_send(new, send_rows, send, dests, peers)


def second_kernel(peers, own, received, successor, weight, dest_at, start_mass,
                  values, p_out, inverse, landed, send, table, flow, *more):
    dests, seg = start_mass.shape
    half = seg // 2
    slots = (table.shape[0] - seg) // peers
    fill(table, own, received, peers, slots, dests)
    gather(table, successor, p_out, dests)
    lane = lax.broadcasted_iota(jnp.int32, (LANES, LANES), 1)
    line = lax.broadcasted_iota(jnp.int32, (LANES, LANES), 0)

    def body(b, weighted):
        at = ds(b * LANES, LANES)
        w = weight[at, :]
        p = p_out[at, :] * w
        p_out[at, :] = p
        parts = []
        for h in range(2):
            here = ds(h * half + b * LANES, LANES)
            mine = (lane >= LANES // 2) == (h == 1)
            x = fold(jnp.where(mine, p, 0.0), dests)
            is_dest = line + (h * half + b * LANES) == dest_at[...]
            v = jnp.where(is_dest, 0.0, jnp.log(x)).T[:dests, :]
            values[:, here] = v
            mass = start_mass[:, here]
            weighted = weighted + mass * v
            inv = jnp.where(is_dest, 0.0, 1.0 / x)
            inverse[here, :] = inv
            parts.append(rows_of(mass) * inv)
        flow[at, :] = jnp.where(lane >= LANES // 2, parts[1], parts[0]) * w
        return weighted

    weighted = lax.fori_loop(0, half // LANES, body, jnp.zeros((dests, LANES), jnp.float32))
    tables = (table,) + more
    scatter(tables, flow, successor, dests)
    finish_spread(tables, seg, peers, slots, landed, send, dests)
    per = slots * dests // LANES

    @pl.loop(0, peers)
    def _(i):
        send[i, pl.ds(per, dests), :] = weighted


def third_kernel(peers, own, received, successor, weight, start_mass, p_in, inverse, landed_in, send_rows,
                 edge_visits, landed, send, total_out, table, flow, inward, *more):
    edges, seg = edge_visits.shape
    slots = send_rows.shape[0] // peers
    half = seg // 2
    dests = LANES // (2 * edges)
    per = slots * dests // LANES
    lane = lax.broadcasted_iota(jnp.int32, (LANES, LANES), 1)

    weighted = jnp.zeros((dests, LANES), jnp.float32)
    for i in range(peers):
        inward[pl.ds(i * per, per), :] = received[i, :per, :]
        weighted = weighted + received[i, per:, :]
    total_out[...] = jnp.broadcast_to(jnp.sum(weighted, axis=1, keepdims=True), (dests, LANES))

    @pl.loop(0, seg // 64)
    def _(b):
        table[ds(b * 64, 64), :] = landed_in[ds(b * 64, 64), :]

    settle(table, inward, send_rows, dests, peers)

    @pl.loop(0, half // LANES)
    def _(b):
        at = ds(b * LANES, LANES)
        visits, parts = [], []
        for h in range(2):
            here = ds(h * half + b * LANES, LANES)
            mass = own[here, :] * fold(table[here, :], dests)
            inv = inverse[here, :]
            parts.append(mass * inv)
            visits.append((rows_of(start_mass[:, here]) + mass) * inv)
        flow[at, :] = jnp.where(lane >= LANES // 2, parts[1], parts[0]) * weight[at, :]
        seen = jnp.where(lane >= LANES // 2, visits[1], visits[0]) * p_in[at, :]
        seen = seen.T
        lines = [jnp.sum(seen[c * dests : (c + 1) * dests, :], axis=0, keepdims=True) for c in range(2 * edges)]
        for h in range(2):
            edge_visits[:, ds(h * half + b * LANES, LANES)] = jnp.concatenate(
                lines[h * edges : (h + 1) * edges], axis=0
            )

    tables = (table,) + more
    scatter(tables, flow, successor, dests)
    finish_spread(tables, seg, peers, slots, landed, send, dests)


def last_kernel(peers, own, received, landed_in, send_rows, arrival, table):
    dests, seg = arrival.shape

    @pl.loop(0, seg // 64)
    def _(b):
        table[ds(b * 64, 64), :] = landed_in[ds(b * 64, 64), :]

    settle(table, received, send_rows, dests, peers)

    @pl.loop(0, seg // LANES)
    def _(b):
        at = ds(b * LANES, LANES)
        arrival[:, at] = (own[at, :] * fold(table[at, :], dests)).T[:dests, :]


def call(kernel, peers, specs, shapes, scratch, name):
    return pl.pallas_call(
        functools.partial(kernel, peers),
        in_specs=specs,
        out_specs=[VMEM] * len(shapes),
        out_shape=[jax.ShapeDtypeStruct(s, jnp.float32) for s in shapes],
        scratch_shapes=[pltpu.VMEM(s, jnp.float32) for s in scratch],
        compiler_params=pltpu.CompilerParams(vmem_limit_bytes=56 * 1024 * 1024),
        name=name,
    )


def local(successor, send_rows, rewards, value_init, start_mass, dest):
    edges, seg = successor.shape
    _, peers, slots = send_rows.shape
    dests = value_init.shape[0]
    half = seg // 2
    groups = LANES // dests
    per = slots // groups
    all_rows = seg + peers * slots
    dest_at = jnp.tile(dest - lax.axis_index("region") * seg, groups)[None]
    rows, packed, sent = (seg, LANES), (half, LANES), (peers * per, LANES)
    big = (all_rows, LANES)
    more = [big] * (TABLES - 1)
    successor, send_rows = successor.reshape(-1), send_rows.reshape(-1)

    def exchange(x):
        y = lax.all_to_all(
            x.reshape(peers, -1, LANES), "region", split_axis=0, concat_axis=0, tiled=True
        )
        return y.reshape(x.shape)

    zero, send = call(start_kernel, peers, [VMEM, SMEM], [rows, sent], [], "start")(value_init, send_rows)
    one, weight, send = call(
        first_kernel, peers, [VMEM, VMEM, SMEM, VMEM, VMEM, SMEM], [rows, packed, sent], [big, packed], "first"
    )(zero, exchange(send), successor, rewards, dest_at, send_rows)

    values, p, inverse, landed, send = call(
        second_kernel, peers, [VMEM, VMEM, SMEM, VMEM, VMEM, VMEM],
        [(dests, seg), packed, rows, rows, (peers, per + dests, LANES)], [big, packed] + more, "second",
    )(one, exchange(send), successor, weight, dest_at, start_mass)
    edge_visits, landed, send, totals = call(
        third_kernel, peers, [VMEM, VMEM, SMEM, VMEM, VMEM, VMEM, VMEM, VMEM, SMEM],
        [(edges, seg), rows, (peers, per, LANES), (dests, LANES)], [big, packed, sent] + more, "third",
    )(one, exchange(send), successor, weight, start_mass, p, inverse, landed, send_rows)
    (arrival,) = call(last_kernel, peers, [VMEM, VMEM, VMEM, SMEM], [(dests, seg)], [rows], "last")(
        one, exchange(send).reshape(sent), landed, send_rows
    )
    return values, edge_visits, arrival, totals[:, 0]


def solution(mesh):
    placed = (
        P(None, ("groups", "region")),
        P(("groups", "region"), None, None),
        P(None, ("groups", "region")),
        P(None, ("groups", "region")),
        P(None, ("groups", "region")),
        P("groups"),
    )
    return jax.shard_map(
        local,
        mesh=mesh,
        in_specs=placed,
        out_specs=(
            P(None, ("groups", "region")),
            P(None, ("groups", "region")),
            P(None, ("groups", "region")),
            P("groups"),
        ),
        check_vma=False,
    )
```

```python
import functools

import jax
import jax.numpy as jnp
from jax import lax
from jax.experimental import pallas as pl
from jax.experimental.pallas import tpu as pltpu
from jax.sharding import PartitionSpec as P

LANES = 128
VMEM = pl.BlockSpec(memory_space=pltpu.VMEM)
SMEM = pl.BlockSpec(memory_space=pltpu.SMEM)
TABLES = 2


def group_of(rows, dests):
    return lax.broadcasted_iota(jnp.int32, (rows, LANES), 1) // dests


def fold(x, dests):
    shift = dests
    while shift < LANES:
        x = x + pltpu.roll(x, shift, axis=1)
        shift *= 2
    return x


def rows_of(block):
    return jnp.concatenate([block] * (LANES // block.shape[0]), axis=0).T


def ds(start, size):
    return pl.ds(pl.multiple_of(start, size), size)


def pack_send(table, send_rows, out, dests, peers):
    slots = send_rows.shape[0] // peers
    groups = LANES // dests
    per = slots // groups
    where = group_of(1, dests)

    @pl.loop(0, peers)
    def _(i):
        @pl.loop(0, per, unroll=8)
        def _(r):
            row = table[pl.ds(send_rows[i * slots + r], 1), :]
            for c in range(1, groups):
                other = table[pl.ds(send_rows[i * slots + c * per + r], 1), :]
                row = jnp.where(where == c, other, row)
            out[pl.ds(i * per + r, 1), :] = row


def fill(table, own, received, peers, slots, dests):
    seg = own.shape[0]
    groups = LANES // dests
    per = slots // groups
    where = group_of(per, dests)

    @pl.loop(0, seg // 64, unroll=2)
    def _(b):
        table[ds(b * 64, 64), :] = own[ds(b * 64, 64), :]

    @pl.loop(0, peers)
    def _(i):
        block = received[ds(i * per, per), :]
        for c in range(groups):
            one = fold(jnp.where(where == c, block, 0.0), dests)
            table[ds(seg + i * slots + c * per, per), :] = one


def gather(table, successor, out, dests):
    half = out.shape[0]
    edges = LANES // (2 * dests)
    where = group_of(1, dests)

    @pl.loop(0, half, unroll=8)
    def _(r):
        row = None
        for c in range(2 * edges):
            other = table[pl.ds(successor[(c % edges * 2 + c // edges) * half + r], 1), :]
            row = other if row is None else jnp.where(where == c, other, row)
        out[pl.ds(r, 1), :] = row


def scatter(tables, flow, successor, dests):
    half = flow.shape[0]
    edges = LANES // (2 * dests)
    step = half // len(tables)
    where = group_of(1, dests)

    for table in tables:
        @pl.loop(0, table.shape[0] // 64)
        def _(b):
            table[ds(b * 64, 64), :] = jnp.zeros((64, LANES), jnp.float32)

    @pl.loop(0, step, unroll=2)
    def _(r0):
        work = []
        for n, table in enumerate(tables):
            r = r0 + n * step
            row = flow[pl.ds(r, 1), :]
            for c in range(2 * edges):
                at = table.at[pl.ds(successor[(c % edges * 2 + c // edges) * half + r], 1), :]
                work.append((at, at[...] + row, where == c))
        for at, value, mask in work:
            pltpu.store(at, value, mask=mask)


def settle(table, received, send_rows, dests, peers):
    slots = send_rows.shape[0] // peers
    groups = LANES // dests
    per = slots // groups
    where = group_of(1, dests)

    @pl.loop(0, peers)
    def _(i):
        @pl.loop(0, per, unroll=4)
        def _(r):
            row = received[pl.ds(i * per + r, 1), :]
            work = []
            for c in range(groups):
                at = table.at[pl.ds(send_rows[i * slots + c * per + r], 1), :]
                work.append((at, at[...] + row, where == c))
            for at, value, mask in work:
                pltpu.store(at, value, mask=mask)


def total(tables, rows):
    x = tables[0][rows, :]
    for table in tables[1:]:
        x = x + table[rows, :]
    return x


def finish_spread(tables, seg, peers, slots, own_out, send_out, dests):
    groups = LANES // dests
    per = slots // groups
    where = group_of(per, dests)

    @pl.loop(0, seg // 64, unroll=2)
    def _(b):
        own_out[ds(b * 64, 64), :] = total(tables, ds(b * 64, 64))

    @pl.loop(0, peers)
    def _(i):
        block = None
        for c in range(groups):
            one = fold(total(tables, ds(seg + i * slots + c * per, per)), dests)
            block = one if block is None else jnp.where(where == c, one, block)
        send_out[i, pl.ds(0, per), :] = block


def start_kernel(peers, value, send_rows, table, send):
    dests, seg = value.shape

    @pl.loop(0, seg // LANES, unroll=4)
    def _(b):
        table[ds(b * LANES, LANES), :] = rows_of(jnp.exp(value[:, ds(b * LANES, LANES)]))

    pack_send(table, send_rows, send, dests, peers)


def first_kernel(peers, own, received, successor, rewards, dest_at, send_rows, new, weight, send, table, got):
    edges, seg = rewards.shape
    slots = send_rows.shape[0] // peers
    half = seg // 2
    dests = LANES // (2 * edges)
    fill(table, own, received, peers, slots, dests)
    gather(table, successor, got, dests)
    lane = lax.broadcasted_iota(jnp.int32, (LANES, LANES), 1)
    line = lax.broadcasted_iota(jnp.int32, (LANES, LANES), 0)

    @pl.loop(0, half // LANES, unroll=2)
    def _(b):
        at = ds(b * LANES, LANES)
        both = [jnp.exp(rewards[:, ds(h * half + b * LANES, LANES)]) for h in range(2)]
        lines = [jnp.broadcast_to(x[e : e + 1, :], (dests, LANES)) for x in both for e in range(edges)]
        w = jnp.concatenate(lines, axis=0).T
        weight[at, :] = w
        p = got[at, :] * w
        for h in range(2):
            mine = (lane >= LANES // 2) == (h == 1)
            x = fold(jnp.where(mine, p, 0.0), dests)
            is_dest = line + (h * half + b * LANES) == dest_at[...]
            new[ds(h * half + b * LANES, LANES), :] = jnp.where(is_dest, 1.0, x)

    pack_send(new, send_rows, send, dests, peers)


def second_kernel(peers, own, received, successor, weight, dest_at, start_mass,
                  values, p_out, inverse, landed, send, table, flow, *more):
    dests, seg = start_mass.shape
    half = seg // 2
    slots = (table.shape[0] - seg) // peers
    fill(table, own, received, peers, slots, dests)
    gather(table, successor, p_out, dests)
    lane = lax.broadcasted_iota(jnp.int32, (LANES, LANES), 1)
    line = lax.broadcasted_iota(jnp.int32, (LANES, LANES), 0)

    def body(b, weighted):
        at = ds(b * LANES, LANES)
        w = weight[at, :]
        p = p_out[at, :] * w
        p_out[at, :] = p
        parts = []
        for h in range(2):
            here = ds(h * half + b * LANES, LANES)
            mine = (lane >= LANES // 2) == (h == 1)
            x = fold(jnp.where(mine, p, 0.0), dests)
            is_dest = line + (h * half + b * LANES) == dest_at[...]
            v = jnp.where(is_dest, 0.0, jnp.log(x)).T[:dests, :]
            values[:, here] = v
            mass = start_mass[:, here]
            weighted = weighted + mass * v
            inv = jnp.where(is_dest, 0.0, 1.0 / x)
            inverse[here, :] = inv
            parts.append(rows_of(mass) * inv)
        flow[at, :] = jnp.where(lane >= LANES // 2, parts[1], parts[0]) * w
        return weighted

    weighted = lax.fori_loop(0, half // LANES, body, jnp.zeros((dests, LANES), jnp.float32), unroll=2)
    tables = (table,) + more
    scatter(tables, flow, successor, dests)
    finish_spread(tables, seg, peers, slots, landed, send, dests)
    per = slots * dests // LANES

    @pl.loop(0, peers)
    def _(i):
        send[i, pl.ds(per, dests), :] = weighted


def third_kernel(peers, own, received, successor, weight, start_mass, p_in, inverse, landed_in, send_rows,
                 edge_visits, landed, send, total_out, table, flow, inward, *more):
    edges, seg = edge_visits.shape
    slots = send_rows.shape[0] // peers
    half = seg // 2
    dests = LANES // (2 * edges)
    per = slots * dests // LANES
    lane = lax.broadcasted_iota(jnp.int32, (LANES, LANES), 1)

    weighted = jnp.zeros((dests, LANES), jnp.float32)
    for i in range(peers):
        inward[pl.ds(i * per, per), :] = received[i, :per, :]
        weighted = weighted + received[i, per:, :]
    total_out[...] = jnp.broadcast_to(jnp.sum(weighted, axis=1, keepdims=True), (dests, LANES))

    @pl.loop(0, seg // 64, unroll=2)
    def _(b):
        table[ds(b * 64, 64), :] = landed_in[ds(b * 64, 64), :]

    settle(table, inward, send_rows, dests, peers)

    @pl.loop(0, half // LANES, unroll=2)
    def _(b):
        at = ds(b * LANES, LANES)
        visits, parts = [], []
        for h in range(2):
            here = ds(h * half + b * LANES, LANES)
            mass = own[here, :] * fold(table[here, :], dests)
            inv = inverse[here, :]
            parts.append(mass * inv)
            visits.append((rows_of(start_mass[:, here]) + mass) * inv)
        flow[at, :] = jnp.where(lane >= LANES // 2, parts[1], parts[0]) * weight[at, :]
        seen = jnp.where(lane >= LANES // 2, visits[1], visits[0]) * p_in[at, :]
        seen = seen.T
        lines = [jnp.sum(seen[c * dests : (c + 1) * dests, :], axis=0, keepdims=True) for c in range(2 * edges)]
        for h in range(2):
            edge_visits[:, ds(h * half + b * LANES, LANES)] = jnp.concatenate(
                lines[h * edges : (h + 1) * edges], axis=0
            )

    tables = (table,) + more
    scatter(tables, flow, successor, dests)
    finish_spread(tables, seg, peers, slots, landed, send, dests)


def last_kernel(peers, own, received, landed_in, send_rows, arrival, table):
    dests, seg = arrival.shape

    @pl.loop(0, seg // 64, unroll=2)
    def _(b):
        table[ds(b * 64, 64), :] = landed_in[ds(b * 64, 64), :]

    settle(table, received, send_rows, dests, peers)

    @pl.loop(0, seg // LANES, unroll=4)
    def _(b):
        at = ds(b * LANES, LANES)
        parts = (own[at, :] * table[at, :]).T
        arrival[:, at] = sum(parts[c : c + dests, :] for c in range(0, LANES, dests))


def exchange_kernel(peers, block, out, landing, send_sem, recv_sem):
    me = lax.axis_index("region")
    others = [lax.rem(me + d, peers) for d in range(1, peers)]
    barrier = pltpu.get_barrier_semaphore()
    for other in others:
        pl.semaphore_signal(
            barrier, inc=1, device_id={"region": other}, device_id_type=pl.DeviceIdType.MESH
        )
    pl.semaphore_wait(barrier, peers - 1)
    copies = []
    for d, other in enumerate(others):
        copy = pltpu.make_async_remote_copy(
            src_ref=block.at[other],
            dst_ref=landing.at[me],
            send_sem=send_sem.at[d],
            recv_sem=recv_sem.at[d],
            device_id={"region": other},
            device_id_type=pl.DeviceIdType.MESH,
        )
        copy.start()
        copies.append(copy)
    out[me] = block[me]
    for d, copy in enumerate(copies):
        copy.wait()
        source = lax.rem(me + peers - 1 - d, peers)
        out[source] = landing[source]


def call(kernel, peers, specs, shapes, scratch, name):
    return pl.pallas_call(
        functools.partial(kernel, peers),
        in_specs=specs,
        out_specs=[VMEM] * len(shapes),
        out_shape=[jax.ShapeDtypeStruct(s, jnp.float32) for s in shapes],
        scratch_shapes=[pltpu.VMEM(s, jnp.float32) for s in scratch],
        compiler_params=pltpu.CompilerParams(vmem_limit_bytes=56 * 1024 * 1024),
        name=name,
    )


def local(successor, send_rows, rewards, value_init, start_mass, dest):
    edges, seg = successor.shape
    _, peers, slots = send_rows.shape
    dests = value_init.shape[0]
    half = seg // 2
    groups = LANES // dests
    per = slots // groups
    all_rows = seg + peers * slots
    dest_at = jnp.tile(dest - lax.axis_index("region") * seg, groups)[None]
    rows, packed, sent = (seg, LANES), (half, LANES), (peers * per, LANES)
    big = (all_rows, LANES)
    more = [big] * (TABLES - 1)
    successor, send_rows = successor.reshape(-1), send_rows.reshape(-1)

    def exchange(x, number):
        blocks = (peers, x.size // (peers * LANES), LANES)
        y = pl.pallas_call(
            functools.partial(exchange_kernel, peers),
            in_specs=[VMEM],
            out_specs=VMEM,
            out_shape=jax.ShapeDtypeStruct(blocks, jnp.float32),
            scratch_shapes=[
                pltpu.VMEM(blocks, jnp.float32),
                pltpu.SemaphoreType.DMA((peers,)),
                pltpu.SemaphoreType.DMA((peers,)),
            ],
            compiler_params=pltpu.CompilerParams(collective_id=number, has_side_effects=True),
            name=f"exchange{number}",
        )(x.reshape(blocks))
        return y.reshape(x.shape)

    zero, send = call(start_kernel, peers, [VMEM, SMEM], [rows, sent], [], "start")(value_init, send_rows)
    one, weight, send = call(
        first_kernel, peers, [VMEM, VMEM, SMEM, VMEM, VMEM, SMEM], [rows, packed, sent], [big, packed], "first"
    )(zero, exchange(send, 0), successor, rewards, dest_at, send_rows)

    values, p, inverse, landed, send = call(
        second_kernel, peers, [VMEM, VMEM, SMEM, VMEM, VMEM, VMEM],
        [(dests, seg), packed, rows, rows, (peers, per + dests, LANES)], [big, packed] + more, "second",
    )(one, exchange(send, 1), successor, weight, dest_at, start_mass)
    edge_visits, landed, send, totals = call(
        third_kernel, peers, [VMEM, VMEM, SMEM, VMEM, VMEM, VMEM, VMEM, VMEM, SMEM],
        [(edges, seg), rows, (peers, per, LANES), (dests, LANES)], [big, packed, sent] + more, "third",
    )(one, exchange(send, 2), successor, weight, start_mass, p, inverse, landed, send_rows)
    (arrival,) = call(last_kernel, peers, [VMEM, VMEM, VMEM, SMEM], [(dests, seg)], [rows], "last")(
        one, exchange(send, 3).reshape(sent), landed, send_rows
    )
    return values, edge_visits, arrival, totals[:, 0]


def solution(mesh):
    placed = (
        P(None, ("groups", "region")),
        P(("groups", "region"), None, None),
        P(None, ("groups", "region")),
        P(None, ("groups", "region")),
        P(None, ("groups", "region")),
        P("groups"),
    )
    return jax.shard_map(
        local,
        mesh=mesh,
        in_specs=placed,
        out_specs=(
            P(None, ("groups", "region")),
            P(None, ("groups", "region")),
            P(None, ("groups", "region")),
            P("groups"),
        ),
        check_vma=False,
    )
```

```python
import functools

import jax
import jax.numpy as jnp
from jax import lax
from jax.experimental import pallas as pl
from jax.experimental.pallas import tpu as pltpu
from jax.sharding import PartitionSpec as P

LANES = 128
VMEM = pl.BlockSpec(memory_space=pltpu.VMEM)
SMEM = pl.BlockSpec(memory_space=pltpu.SMEM)
TABLES = 2


def group_of(rows, dests):
    return lax.broadcasted_iota(jnp.int32, (rows, LANES), 1) // dests


def fold(x, dests):
    shift = dests
    while shift < LANES:
        x = x + pltpu.roll(x, shift, axis=1)
        shift *= 2
    return x


def rows_of(block):
    return jnp.concatenate([block] * (LANES // block.shape[0]), axis=0).T


def ds(start, size):
    return pl.ds(pl.multiple_of(start, size), size)


def exchange_table(table, send_rows, send, landing, send_sem, recv_sem, dests, ready):
    peers, per, _ = send.shape
    groups = LANES // dests
    slots = groups * per
    seg = table.shape[0] - peers * slots
    where, wide = group_of(1, dests), group_of(per, dests)
    me = lax.axis_index("region")

    def pack(i):
        @pl.loop(0, per, unroll=8)
        def _(r):
            row = table[pl.ds(send_rows[i * slots + r], 1), :]
            for c in range(1, groups):
                other = table[pl.ds(send_rows[i * slots + c * per + r], 1), :]
                row = jnp.where(where == c, other, row)
            send[i, pl.ds(r, 1), :] = row

    def unpack(i, block):
        for c in range(groups):
            one = fold(jnp.where(wide == c, block, 0.0), dests)
            table[ds(seg + i * slots + c * per, per), :] = one

    copies = []
    for d in range(1, peers):
        other = lax.rem(me + d, peers)
        pack(other)
        if d == 1:
            ready()
        copy = pltpu.make_async_remote_copy(
            src_ref=send.at[other],
            dst_ref=landing.at[me],
            send_sem=send_sem.at[d],
            recv_sem=recv_sem.at[d],
            device_id={"region": other},
            device_id_type=pl.DeviceIdType.MESH,
        )
        copy.start()
        copies.append(copy)
    pack(me)
    unpack(me, send[me])
    for d, copy in enumerate(copies):
        copy.wait()
        source = lax.rem(me + peers - 1 - d, peers)
        unpack(source, landing[source])


def gather(table, successor, out, dests):
    half = out.shape[0]
    edges = LANES // (2 * dests)
    where = group_of(1, dests)

    @pl.loop(0, half, unroll=16)
    def _(r):
        row = None
        for c in range(2 * edges):
            other = table[pl.ds(successor[(c % edges * 2 + c // edges) * half + r], 1), :]
            row = other if row is None else jnp.where(where == c, other, row)
        out[pl.ds(r, 1), :] = row


def scatter(tables, flow, successor, dests):
    half = flow.shape[0]
    edges = LANES // (2 * dests)
    step = half // len(tables)
    where = group_of(1, dests)

    for table in tables:
        @pl.loop(0, table.shape[0] // 64)
        def _(b):
            table[ds(b * 64, 64), :] = jnp.zeros((64, LANES), jnp.float32)

    @pl.loop(0, step, unroll=4)
    def _(r0):
        work = []
        for n, table in enumerate(tables):
            r = r0 + n * step
            row = flow[pl.ds(r, 1), :]
            for c in range(2 * edges):
                at = table.at[pl.ds(successor[(c % edges * 2 + c // edges) * half + r], 1), :]
                work.append((at, at[...] + row, where == c))
        for at, value, mask in work:
            pltpu.store(at, value, mask=mask)


def settle(table, received, send_rows, dests, peers):
    slots = send_rows.shape[0] // peers
    groups = LANES // dests
    per = slots // groups
    where = group_of(1, dests)

    @pl.loop(0, peers)
    def _(i):
        @pl.loop(0, per, unroll=4)
        def _(r):
            row = received[pl.ds(i * per + r, 1), :]
            work = []
            for c in range(groups):
                at = table.at[pl.ds(send_rows[i * slots + c * per + r], 1), :]
                work.append((at, at[...] + row, where == c))
            for at, value, mask in work:
                pltpu.store(at, value, mask=mask)


def total(tables, rows):
    x = tables[0][rows, :]
    for table in tables[1:]:
        x = x + table[rows, :]
    return x


def finish_spread(tables, seg, peers, slots, own_out, send_out, dests):
    groups = LANES // dests
    per = slots // groups
    where = group_of(per, dests)

    @pl.loop(0, seg // 64, unroll=2)
    def _(b):
        own_out[ds(b * 64, 64), :] = total(tables, ds(b * 64, 64))

    @pl.loop(0, peers)
    def _(i):
        block = None
        for c in range(groups):
            one = fold(total(tables, ds(seg + i * slots + c * per, per)), dests)
            block = one if block is None else jnp.where(where == c, one, block)
        send_out[i, pl.ds(0, per), :] = block


def backup_kernel(peers, value, send_rows, successor, rewards, dest_at, start_mass,
                  one, weight, values, p_out, inverse, flow, weighted_out,
                  table, send, landing, send_again, landing_again, send_sem, recv_sem, send_sem_again, recv_sem_again):
    dests, seg = value.shape
    edges = rewards.shape[0]
    half = seg // 2
    me = lax.axis_index("region")
    barrier = pltpu.get_barrier_semaphore()
    for d in range(1, peers):
        pl.semaphore_signal(
            barrier, inc=1, device_id={"region": lax.rem(me + d, peers)}, device_id_type=pl.DeviceIdType.MESH
        )

    @pl.loop(0, seg // LANES, unroll=4)
    def _(b):
        table[ds(b * LANES, LANES), :] = rows_of(jnp.exp(value[:, ds(b * LANES, LANES)]))

    exchange_table(
        table, send_rows, send, landing, send_sem, recv_sem, dests,
        lambda: pl.semaphore_wait(barrier, peers - 1),
    )
    gather(table, successor, p_out, dests)
    lane = lax.broadcasted_iota(jnp.int32, (LANES, LANES), 1)
    line = lax.broadcasted_iota(jnp.int32, (LANES, LANES), 0)

    @pl.loop(0, half // LANES, unroll=2)
    def _(b):
        at = ds(b * LANES, LANES)
        both = [jnp.exp(rewards[:, ds(h * half + b * LANES, LANES)]) for h in range(2)]
        lines = [jnp.broadcast_to(x[e : e + 1, :], (dests, LANES)) for x in both for e in range(edges)]
        w = jnp.concatenate(lines, axis=0).T
        weight[at, :] = w
        p = p_out[at, :] * w
        for h in range(2):
            here = ds(h * half + b * LANES, LANES)
            mine = (lane >= LANES // 2) == (h == 1)
            x = fold(jnp.where(mine, p, 0.0), dests)
            is_dest = line + (h * half + b * LANES) == dest_at[...]
            x = jnp.where(is_dest, 1.0, x)
            table[here, :] = x
            one[here, :] = x

    exchange_table(
        table, send_rows, send_again, landing_again, send_sem_again, recv_sem_again, dests, lambda: None
    )
    gather(table, successor, p_out, dests)

    def body(b, weighted):
        at = ds(b * LANES, LANES)
        w = weight[at, :]
        p = p_out[at, :] * w
        p_out[at, :] = p
        parts = []
        for h in range(2):
            here = ds(h * half + b * LANES, LANES)
            mine = (lane >= LANES // 2) == (h == 1)
            x = fold(jnp.where(mine, p, 0.0), dests)
            is_dest = line + (h * half + b * LANES) == dest_at[...]
            v = jnp.where(is_dest, 0.0, jnp.log(x)).T[:dests, :]
            values[:, here] = v
            mass = start_mass[:, here]
            weighted = weighted + mass * v
            inv = jnp.where(is_dest, 0.0, 1.0 / x)
            inverse[here, :] = inv
            parts.append(rows_of(mass) * inv)
        flow[at, :] = jnp.where(lane >= LANES // 2, parts[1], parts[0]) * w
        return weighted

    weighted_out[...] = lax.fori_loop(
        0, half // LANES, body, jnp.zeros((dests, LANES), jnp.float32), unroll=2
    )


def push_kernel(peers, flow, successor, weighted, landed, send, *tables):
    dests = weighted.shape[0]
    seg = landed.shape[0]
    slots = (tables[0].shape[0] - seg) // peers
    per = slots * dests // LANES
    scatter(tables, flow, successor, dests)
    finish_spread(tables, seg, peers, slots, landed, send, dests)

    @pl.loop(0, peers)
    def _(i):
        send[i, pl.ds(per, dests), :] = weighted[...]


def third_kernel(peers, own, received, successor, weight, start_mass, p_in, inverse, landed_in, send_rows,
                 edge_visits, landed, send, total_out, table, flow, inward, *more):
    edges, seg = edge_visits.shape
    slots = send_rows.shape[0] // peers
    half = seg // 2
    dests = LANES // (2 * edges)
    per = slots * dests // LANES
    lane = lax.broadcasted_iota(jnp.int32, (LANES, LANES), 1)

    weighted = jnp.zeros((dests, LANES), jnp.float32)
    for i in range(peers):
        inward[pl.ds(i * per, per), :] = received[i, :per, :]
        weighted = weighted + received[i, per:, :]
    total_out[...] = jnp.broadcast_to(jnp.sum(weighted, axis=1, keepdims=True), (dests, LANES))

    @pl.loop(0, seg // 64, unroll=2)
    def _(b):
        table[ds(b * 64, 64), :] = landed_in[ds(b * 64, 64), :]

    settle(table, inward, send_rows, dests, peers)

    @pl.loop(0, half // LANES, unroll=2)
    def _(b):
        at = ds(b * LANES, LANES)
        visits, parts = [], []
        for h in range(2):
            here = ds(h * half + b * LANES, LANES)
            mass = own[here, :] * fold(table[here, :], dests)
            inv = inverse[here, :]
            parts.append(mass * inv)
            visits.append((rows_of(start_mass[:, here]) + mass) * inv)
        flow[at, :] = jnp.where(lane >= LANES // 2, parts[1], parts[0]) * weight[at, :]
        seen = jnp.where(lane >= LANES // 2, visits[1], visits[0]) * p_in[at, :]
        seen = seen.T
        lines = [jnp.sum(seen[c * dests : (c + 1) * dests, :], axis=0, keepdims=True) for c in range(2 * edges)]
        for h in range(2):
            edge_visits[:, ds(h * half + b * LANES, LANES)] = jnp.concatenate(
                lines[h * edges : (h + 1) * edges], axis=0
            )

    tables = (table,) + more
    scatter(tables, flow, successor, dests)
    finish_spread(tables, seg, peers, slots, landed, send, dests)


def last_kernel(peers, own, received, landed_in, send_rows, arrival, table):
    dests, seg = arrival.shape

    @pl.loop(0, seg // 64, unroll=2)
    def _(b):
        table[ds(b * 64, 64), :] = landed_in[ds(b * 64, 64), :]

    settle(table, received, send_rows, dests, peers)

    @pl.loop(0, seg // LANES, unroll=4)
    def _(b):
        at = ds(b * LANES, LANES)
        parts = (own[at, :] * table[at, :]).T
        arrival[:, at] = sum(parts[c : c + dests, :] for c in range(0, LANES, dests))


def exchange_kernel(peers, block, out, landing, send_sem, recv_sem):
    me = lax.axis_index("region")
    others = [lax.rem(me + d, peers) for d in range(1, peers)]
    barrier = pltpu.get_barrier_semaphore()
    for other in others:
        pl.semaphore_signal(
            barrier, inc=1, device_id={"region": other}, device_id_type=pl.DeviceIdType.MESH
        )
    pl.semaphore_wait(barrier, peers - 1)
    copies = []
    for d, other in enumerate(others):
        copy = pltpu.make_async_remote_copy(
            src_ref=block.at[other],
            dst_ref=landing.at[me],
            send_sem=send_sem.at[d],
            recv_sem=recv_sem.at[d],
            device_id={"region": other},
            device_id_type=pl.DeviceIdType.MESH,
        )
        copy.start()
        copies.append(copy)
    out[me] = block[me]
    for d, copy in enumerate(copies):
        copy.wait()
        source = lax.rem(me + peers - 1 - d, peers)
        out[source] = landing[source]


def call(kernel, peers, specs, shapes, scratch, name):
    return pl.pallas_call(
        functools.partial(kernel, peers),
        in_specs=specs,
        out_specs=[VMEM] * len(shapes),
        out_shape=[jax.ShapeDtypeStruct(s, jnp.float32) for s in shapes],
        scratch_shapes=[pltpu.VMEM(s, jnp.float32) for s in scratch],
        compiler_params=pltpu.CompilerParams(vmem_limit_bytes=56 * 1024 * 1024),
        name=name,
    )


def local(successor, send_rows, rewards, value_init, start_mass, dest):
    edges, seg = successor.shape
    _, peers, slots = send_rows.shape
    dests = value_init.shape[0]
    half = seg // 2
    groups = LANES // dests
    per = slots // groups
    all_rows = seg + peers * slots
    dest_at = jnp.tile(dest - lax.axis_index("region") * seg, groups)[None]
    rows, packed, sent = (seg, LANES), (half, LANES), (peers * per, LANES)
    big = (all_rows, LANES)
    more = [big] * (TABLES - 1)
    successor, send_rows = successor.reshape(-1), send_rows.reshape(-1)

    def exchange(x, number):
        blocks = (peers, x.size // (peers * LANES), LANES)
        y = pl.pallas_call(
            functools.partial(exchange_kernel, peers),
            in_specs=[VMEM],
            out_specs=VMEM,
            out_shape=jax.ShapeDtypeStruct(blocks, jnp.float32),
            scratch_shapes=[
                pltpu.VMEM(blocks, jnp.float32),
                pltpu.SemaphoreType.DMA((peers,)),
                pltpu.SemaphoreType.DMA((peers,)),
            ],
            compiler_params=pltpu.CompilerParams(collective_id=number, has_side_effects=True),
            name=f"exchange{number}",
        )(x.reshape(blocks))
        return y.reshape(x.shape)

    blocks = (peers, per, LANES)
    one, weight, values, p, inverse, flow, weighted = pl.pallas_call(
        functools.partial(backup_kernel, peers),
        in_specs=[VMEM, SMEM, SMEM, VMEM, VMEM, VMEM],
        out_specs=[VMEM] * 7,
        out_shape=[
            jax.ShapeDtypeStruct(x, jnp.float32)
            for x in (rows, packed, (dests, seg), packed, rows, packed, (dests, LANES))
        ],
        scratch_shapes=[pltpu.VMEM(big, jnp.float32)]
        + [pltpu.VMEM(blocks, jnp.float32)] * 4
        + [pltpu.SemaphoreType.DMA((peers,))] * 4,
        compiler_params=pltpu.CompilerParams(
            collective_id=0, has_side_effects=True, vmem_limit_bytes=56 * 1024 * 1024
        ),
        name="backup",
    )(value_init, send_rows, successor, rewards, dest_at, start_mass)
    landed, send = call(
        push_kernel, peers, [VMEM, SMEM, VMEM], [rows, (peers, per + dests, LANES)], [big] + more, "push"
    )(flow, successor, weighted)
    edge_visits, landed, send, totals = call(
        third_kernel, peers, [VMEM, VMEM, SMEM, VMEM, VMEM, VMEM, VMEM, VMEM, SMEM],
        [(edges, seg), rows, (peers, per, LANES), (dests, LANES)], [big, packed, sent] + more, "third",
    )(one, exchange(send, 2), successor, weight, start_mass, p, inverse, landed, send_rows)
    (arrival,) = call(last_kernel, peers, [VMEM, VMEM, VMEM, SMEM], [(dests, seg)], [rows], "last")(
        one, exchange(send, 3).reshape(sent), landed, send_rows
    )
    return values, edge_visits, arrival, totals[:, 0]


def solution(mesh):
    placed = (
        P(None, ("groups", "region")),
        P(("groups", "region"), None, None),
        P(None, ("groups", "region")),
        P(None, ("groups", "region")),
        P(None, ("groups", "region")),
        P("groups"),
    )
    return jax.shard_map(
        local,
        mesh=mesh,
        in_specs=placed,
        out_specs=(
            P(None, ("groups", "region")),
            P(None, ("groups", "region")),
            P(None, ("groups", "region")),
            P("groups"),
        ),
        check_vma=False,
    )
```

```python
import functools

import jax
import jax.numpy as jnp
from jax import lax
from jax.experimental import pallas as pl
from jax.experimental.pallas import tpu as pltpu
from jax.sharding import PartitionSpec as P

LANES = 128
VMEM = pl.BlockSpec(memory_space=pltpu.VMEM)
SMEM = pl.BlockSpec(memory_space=pltpu.SMEM)
TABLES = 2


def group_of(rows, dests):
    return lax.broadcasted_iota(jnp.int32, (rows, LANES), 1) // dests


def fold(x, dests):
    shift = dests
    while shift < LANES:
        x = x + pltpu.roll(x, shift, axis=1)
        shift *= 2
    return x


def rows_of(block):
    return jnp.concatenate([block] * (LANES // block.shape[0]), axis=0).T


def ds(start, size):
    return pl.ds(pl.multiple_of(start, size), size)


def exchange_table(table, send_rows, send, landing, send_sem, recv_sem, dests, ready):
    peers, per, _ = send.shape
    groups = LANES // dests
    slots = groups * per
    seg = table.shape[0] - peers * slots
    where, wide = group_of(1, dests), group_of(per, dests)
    me = lax.axis_index("region")

    def pack(i):
        @pl.loop(0, per, unroll=8)
        def _(r):
            row = table[pl.ds(send_rows[i * slots + r], 1), :]
            for c in range(1, groups):
                other = table[pl.ds(send_rows[i * slots + c * per + r], 1), :]
                row = jnp.where(where == c, other, row)
            send[i, pl.ds(r, 1), :] = row

    def unpack(i, block):
        for c in range(groups):
            one = fold(jnp.where(wide == c, block, 0.0), dests)
            table[ds(seg + i * slots + c * per, per), :] = one

    copies = []
    for d in range(1, peers):
        other = lax.rem(me + d, peers)
        pack(other)
        if d == 1:
            ready()
        copy = pltpu.make_async_remote_copy(
            src_ref=send.at[other],
            dst_ref=landing.at[me],
            send_sem=send_sem.at[d],
            recv_sem=recv_sem.at[d],
            device_id={"region": other},
            device_id_type=pl.DeviceIdType.MESH,
        )
        copy.start()
        copies.append(copy)
    pack(me)
    unpack(me, send[me])
    for d, copy in enumerate(copies):
        copy.wait()
        source = lax.rem(me + peers - 1 - d, peers)
        unpack(source, landing[source])


def gather(table, successor, out, dests):
    half = out.shape[0]
    edges = LANES // (2 * dests)
    where = group_of(1, dests)

    @pl.loop(0, half, unroll=16)
    def _(r):
        row = None
        for c in range(2 * edges):
            other = table[pl.ds(successor[(c % edges * 2 + c // edges) * half + r], 1), :]
            row = other if row is None else jnp.where(where == c, other, row)
        out[pl.ds(r, 1), :] = row


def scatter(tables, flow, successor, dests):
    half = flow.shape[0]
    edges = LANES // (2 * dests)
    step = half // len(tables)
    where = group_of(1, dests)

    for table in tables:
        @pl.loop(0, table.shape[0] // 64)
        def _(b):
            table[ds(b * 64, 64), :] = jnp.zeros((64, LANES), jnp.float32)

    @pl.loop(0, step, unroll=4)
    def _(r0):
        work = []
        for n, table in enumerate(tables):
            r = r0 + n * step
            row = flow[pl.ds(r, 1), :]
            for c in range(2 * edges):
                at = table.at[pl.ds(successor[(c % edges * 2 + c // edges) * half + r], 1), :]
                work.append((at, at[...] + row, where == c))
        for at, value, mask in work:
            pltpu.store(at, value, mask=mask)


def settle(table, received, send_rows, dests, peers):
    slots = send_rows.shape[0] // peers
    groups = LANES // dests
    per = slots // groups
    where = group_of(1, dests)

    @pl.loop(0, peers)
    def _(i):
        @pl.loop(0, per, unroll=4)
        def _(r):
            row = received[pl.ds(i * per + r, 1), :]
            work = []
            for c in range(groups):
                at = table.at[pl.ds(send_rows[i * slots + c * per + r], 1), :]
                work.append((at, at[...] + row, where == c))
            for at, value, mask in work:
                pltpu.store(at, value, mask=mask)


def total(tables, rows):
    x = tables[0][rows, :]
    for table in tables[1:]:
        x = x + table[rows, :]
    return x


def finish_spread(tables, seg, peers, slots, own_out, send_out, dests):
    groups = LANES // dests
    per = slots // groups
    where = group_of(per, dests)

    @pl.loop(0, seg // 64, unroll=2)
    def _(b):
        own_out[ds(b * 64, 64), :] = total(tables, ds(b * 64, 64))

    @pl.loop(0, peers)
    def _(i):
        block = None
        for c in range(groups):
            one = fold(total(tables, ds(seg + i * slots + c * per, per)), dests)
            block = one if block is None else jnp.where(where == c, one, block)
        send_out[i, pl.ds(0, per), :] = block


def backup_kernel(peers, value, send_rows, successor, rewards, dest_at, start_mass,
                  one, share, values, p_out, flow, weighted_out,
                  table, weight, send, landing, send_again, landing_again, send_sem, recv_sem, send_sem_again, recv_sem_again):
    dests, seg = value.shape
    edges = rewards.shape[0]
    half = seg // 2
    me = lax.axis_index("region")
    barrier = pltpu.get_barrier_semaphore()
    for d in range(1, peers):
        pl.semaphore_signal(
            barrier, inc=1, device_id={"region": lax.rem(me + d, peers)}, device_id_type=pl.DeviceIdType.MESH
        )

    @pl.loop(0, seg // LANES, unroll=4)
    def _(b):
        table[ds(b * LANES, LANES), :] = rows_of(jnp.exp(value[:, ds(b * LANES, LANES)]))

    exchange_table(
        table, send_rows, send, landing, send_sem, recv_sem, dests,
        lambda: pl.semaphore_wait(barrier, peers - 1),
    )
    gather(table, successor, p_out, dests)
    lane = lax.broadcasted_iota(jnp.int32, (LANES, LANES), 1)
    line = lax.broadcasted_iota(jnp.int32, (LANES, LANES), 0)

    @pl.loop(0, half // LANES, unroll=2)
    def _(b):
        at = ds(b * LANES, LANES)
        both = [jnp.exp(rewards[:, ds(h * half + b * LANES, LANES)]) for h in range(2)]
        lines = [jnp.broadcast_to(x[e : e + 1, :], (dests, LANES)) for x in both for e in range(edges)]
        w = jnp.concatenate(lines, axis=0).T
        weight[at, :] = w
        p = p_out[at, :] * w
        for h in range(2):
            here = ds(h * half + b * LANES, LANES)
            mine = (lane >= LANES // 2) == (h == 1)
            x = fold(jnp.where(mine, p, 0.0), dests)
            is_dest = line + (h * half + b * LANES) == dest_at[...]
            x = jnp.where(is_dest, 1.0, x)
            table[here, :] = x
            one[here, :] = x

    exchange_table(
        table, send_rows, send_again, landing_again, send_sem_again, recv_sem_again, dests, lambda: None
    )
    gather(table, successor, p_out, dests)

    def body(b, weighted):
        at = ds(b * LANES, LANES)
        w = weight[at, :]
        p = p_out[at, :] * w
        starts, inverses = [], []
        for h in range(2):
            here = ds(h * half + b * LANES, LANES)
            mine = (lane >= LANES // 2) == (h == 1)
            x = fold(jnp.where(mine, p, 0.0), dests)
            is_dest = line + (h * half + b * LANES) == dest_at[...]
            v = jnp.where(is_dest, 0.0, jnp.log(x)).T[:dests, :]
            values[:, here] = v
            mass = start_mass[:, here]
            weighted = weighted + mass * v
            inverses.append(jnp.where(is_dest, 0.0, 1.0 / x))
            starts.append(rows_of(mass))
        inv = jnp.where(lane >= LANES // 2, inverses[1], inverses[0])
        p_out[at, :] = p * inv
        share[at, :] = w * inv
        flow[at, :] = jnp.where(lane >= LANES // 2, starts[1], starts[0]) * (w * inv)
        return weighted

    weighted_out[...] = lax.fori_loop(
        0, half // LANES, body, jnp.zeros((dests, LANES), jnp.float32), unroll=2
    )


def push_kernel(peers, flow, successor, weighted, landed, send, *tables):
    dests = weighted.shape[0]
    seg = landed.shape[0]
    slots = (tables[0].shape[0] - seg) // peers
    per = slots * dests // LANES
    scatter(tables, flow, successor, dests)
    finish_spread(tables, seg, peers, slots, landed, send, dests)

    @pl.loop(0, peers)
    def _(i):
        send[i, pl.ds(per, dests), :] = weighted[...]


def third_kernel(peers, own, received, successor, share, landed_in, send_rows,
                 mass_out, landed, send, total_out, table, flow, inward, *more):
    seg = own.shape[0]
    slots = send_rows.shape[0] // peers
    half = seg // 2
    dests = total_out.shape[0]
    per = slots * dests // LANES
    lane = lax.broadcasted_iota(jnp.int32, (LANES, LANES), 1)

    weighted = jnp.zeros((dests, LANES), jnp.float32)
    for i in range(peers):
        inward[pl.ds(i * per, per), :] = received[i, :per, :]
        weighted = weighted + received[i, per:, :]
    total_out[...] = jnp.broadcast_to(jnp.sum(weighted, axis=1, keepdims=True), (dests, LANES))

    @pl.loop(0, seg // 64, unroll=2)
    def _(b):
        table[ds(b * 64, 64), :] = landed_in[ds(b * 64, 64), :]

    settle(table, inward, send_rows, dests, peers)

    @pl.loop(0, half // LANES, unroll=2)
    def _(b):
        at = ds(b * LANES, LANES)
        parts = []
        for h in range(2):
            here = ds(h * half + b * LANES, LANES)
            parts.append(own[here, :] * fold(table[here, :], dests))
        mass = jnp.where(lane >= LANES // 2, parts[1], parts[0])
        mass_out[at, :] = mass
        flow[at, :] = mass * share[at, :]

    tables = (table,) + more
    scatter(tables, flow, successor, dests)
    finish_spread(tables, seg, peers, slots, landed, send, dests)


def last_kernel(peers, own, received, landed_in, send_rows, arrival, table):
    dests, seg = arrival.shape

    @pl.loop(0, seg // 64, unroll=2)
    def _(b):
        table[ds(b * 64, 64), :] = landed_in[ds(b * 64, 64), :]

    settle(table, received, send_rows, dests, peers)

    @pl.loop(0, seg // LANES, unroll=4)
    def _(b):
        at = ds(b * LANES, LANES)
        parts = (own[at, :] * table[at, :]).T
        arrival[:, at] = sum(parts[c : c + dests, :] for c in range(0, LANES, dests))


def visits_part(start_mass, mass, policy, edge_visits):
    edges, seg = edge_visits.shape
    dests = start_mass.shape[0]
    half = seg // 2
    lane = lax.broadcasted_iota(jnp.int32, (LANES, LANES), 1)

    @pl.loop(0, half // LANES, unroll=2)
    def _(b):
        at = ds(b * LANES, LANES)
        low, high = [rows_of(start_mass[:, ds(h * half + b * LANES, LANES)]) for h in range(2)]
        seen = ((jnp.where(lane >= LANES // 2, high, low) + mass[at, :]) * policy[at, :]).T
        lines = [jnp.sum(seen[c * dests : (c + 1) * dests, :], axis=0, keepdims=True) for c in range(2 * edges)]
        for h in range(2):
            edge_visits[:, ds(h * half + b * LANES, LANES)] = jnp.concatenate(
                lines[h * edges : (h + 1) * edges], axis=0
            )


def exchange_visits_kernel(peers, block, start_mass, mass, policy, out, edge_visits, *rest):
    exchange_kernel(peers, block, out, *rest, beside=lambda: visits_part(start_mass, mass, policy, edge_visits))


def exchange_kernel(peers, block, out, landing, send_sem, recv_sem, beside=None):
    me = lax.axis_index("region")
    others = [lax.rem(me + d, peers) for d in range(1, peers)]
    barrier = pltpu.get_barrier_semaphore()
    for other in others:
        pl.semaphore_signal(
            barrier, inc=1, device_id={"region": other}, device_id_type=pl.DeviceIdType.MESH
        )
    pl.semaphore_wait(barrier, peers - 1)
    copies = []
    for d, other in enumerate(others):
        copy = pltpu.make_async_remote_copy(
            src_ref=block.at[other],
            dst_ref=landing.at[me],
            send_sem=send_sem.at[d],
            recv_sem=recv_sem.at[d],
            device_id={"region": other},
            device_id_type=pl.DeviceIdType.MESH,
        )
        copy.start()
        copies.append(copy)
    out[me] = block[me]
    if beside is not None:
        beside()
    for d, copy in enumerate(copies):
        copy.wait()
        source = lax.rem(me + peers - 1 - d, peers)
        out[source] = landing[source]


def call(kernel, peers, specs, shapes, scratch, name):
    return pl.pallas_call(
        functools.partial(kernel, peers),
        in_specs=specs,
        out_specs=[VMEM] * len(shapes),
        out_shape=[jax.ShapeDtypeStruct(s, jnp.float32) for s in shapes],
        scratch_shapes=[pltpu.VMEM(s, jnp.float32) for s in scratch],
        compiler_params=pltpu.CompilerParams(vmem_limit_bytes=56 * 1024 * 1024),
        name=name,
    )


def local(successor, send_rows, rewards, value_init, start_mass, dest):
    edges, seg = successor.shape
    _, peers, slots = send_rows.shape
    dests = value_init.shape[0]
    half = seg // 2
    groups = LANES // dests
    per = slots // groups
    all_rows = seg + peers * slots
    dest_at = jnp.tile(dest - lax.axis_index("region") * seg, groups)[None]
    rows, packed, sent = (seg, LANES), (half, LANES), (peers * per, LANES)
    big = (all_rows, LANES)
    more = [big] * (TABLES - 1)
    successor, send_rows = successor.reshape(-1), send_rows.reshape(-1)

    def exchange(x, number, kernel, *beside, extra=()):
        outs = [x.shape, *extra]
        return pl.pallas_call(
            functools.partial(kernel, peers),
            in_specs=[VMEM] * (1 + len(beside)),
            out_specs=[VMEM] * len(outs),
            out_shape=[jax.ShapeDtypeStruct(o, jnp.float32) for o in outs],
            scratch_shapes=[
                pltpu.VMEM(x.shape, jnp.float32),
                pltpu.SemaphoreType.DMA((peers,)),
                pltpu.SemaphoreType.DMA((peers,)),
            ],
            compiler_params=pltpu.CompilerParams(
                collective_id=number, has_side_effects=True, vmem_limit_bytes=40 * 1024 * 1024
            ),
            name=f"exchange{number}",
        )(x, *beside)

    blocks = (peers, per, LANES)
    one, share, values, policy, flow, weighted = pl.pallas_call(
        functools.partial(backup_kernel, peers),
        in_specs=[VMEM, SMEM, SMEM, VMEM, VMEM, VMEM],
        out_specs=[VMEM] * 6,
        out_shape=[
            jax.ShapeDtypeStruct(x, jnp.float32)
            for x in (rows, packed, (dests, seg), packed, packed, (dests, LANES))
        ],
        scratch_shapes=[pltpu.VMEM(big, jnp.float32), pltpu.VMEM(packed, jnp.float32)]
        + [pltpu.VMEM(blocks, jnp.float32)] * 4
        + [pltpu.SemaphoreType.DMA((peers,))] * 4,
        compiler_params=pltpu.CompilerParams(
            collective_id=0, has_side_effects=True, vmem_limit_bytes=56 * 1024 * 1024
        ),
        name="backup",
    )(value_init, send_rows, successor, rewards, dest_at, start_mass)
    landed, send = call(
        push_kernel, peers, [VMEM, SMEM, VMEM], [rows, (peers, per + dests, LANES)], [big] + more, "push"
    )(flow, successor, weighted)
    (received,) = exchange(send, 2, exchange_kernel)
    mass, landed, send, totals = call(
        third_kernel, peers, [VMEM, VMEM, SMEM, VMEM, VMEM, SMEM],
        [packed, rows, blocks, (dests, LANES)], [big, packed, sent] + more, "third",
    )(one, received, successor, share, landed, send_rows)
    received, edge_visits = exchange(
        send, 3, exchange_visits_kernel, start_mass, mass, policy, extra=[(edges, seg)]
    )
    (arrival,) = call(last_kernel, peers, [VMEM, VMEM, VMEM, SMEM], [(dests, seg)], [rows], "last")(
        one, received.reshape(sent), landed, send_rows
    )
    return values, edge_visits, arrival, totals[:, 0]


def solution(mesh):
    placed = (
        P(None, ("groups", "region")),
        P(("groups", "region"), None, None),
        P(None, ("groups", "region")),
        P(None, ("groups", "region")),
        P(None, ("groups", "region")),
        P("groups"),
    )
    return jax.shard_map(
        local,
        mesh=mesh,
        in_specs=placed,
        out_specs=(
            P(None, ("groups", "region")),
            P(None, ("groups", "region")),
            P(None, ("groups", "region")),
            P("groups"),
        ),
        check_vma=False,
    )
```
